512 devices in a mesh: tm: 64 (over x, z, core), space: 8 (over y).
Axes of the slice: x: 4, y: 8, z: 8, core: 2. Of those that a mesh axis runs over, the one named last changes fastest.
Arguments:
- snapshots: bfloat16 [512, 5, 65536], P('tm', None, 'space'), may hold values from -210 to 210, as said below
- basis: bfloat16 [2, 33, 16, 5, 65536], P(None, None, None, None, ('space', 'tm')), may hold values from -6 to 6
- mass_table: float32 [8, 64, 64], replicated, may hold values from -0.03 to 3, as said below
- elem_kind: int32 [1024], P(('space', 'tm')), may hold values from 0 to 7
- offsets: int32 [8], replicated, may hold values from 0 to 256, as said below
Outputs:
- coeffs: float32 [2, 33, 8, 16], replicated
- new_basis: bfloat16 [2, 33, 16, 5, 65536], P(None, None, None, None, ('space', 'tm'))
The draws below stay inside these ranges and needn't reach their ends.
Inputs may be any that keep to these rules, and one draw needn't show every extreme that they name: `snapshots`: rows of flow data. `mass_table`: each block is symmetric and positive definite. `offsets`: some block starts at 0 and some at 256.
All inputs are finite; a program needn't handle non-finite values.
Results may differ from the reference program's by a relative error of at most 0.0095.
Values may be sent and summed in bfloat16 or wider, within the bound.
No kernel may reach another device: no remote copies, remote signals or barrier semaphores. Data moves between devices by JAX's collectives and lax.ppermute only.
A program may use at most 64 MiB of HBM per device.

```python
import math
import jax
import jax.numpy as jnp
from jax import lax

NVAR = 5
NT = 256
F = 33
RANK = 16
ELEM_PTS = 64
KINDS = 8
RECORD = 512
NB = 8
PD = 128
NPTS = 65536
ELEMS = 1024
N_TM = 64
N_SPACE = 8


def draw_snapshots(key, part):
    key_noise, key_scale = jax.random.split(key, 2)
    point_idx = jnp.arange(NPTS, dtype=jnp.int32)
    tm_pos = (point_idx // PD % N_TM).astype(jnp.float32) / max(N_TM - 1, 1)
    space_pos = (point_idx // (PD * N_TM)).astype(jnp.float32) / max(N_SPACE - 1, 1)
    noise = jax.random.normal(key_noise, (RECORD, NVAR, NPTS), jnp.float32)
    ramp = 1.0 + 1.2 * tm_pos + 0.6 * space_pos
    noise = jnp.clip(noise, -6.0, 6.0)
    spread = jnp.exp(jax.random.uniform(key_scale, (1, NVAR, NPTS), jnp.float32, 0.0, math.log(10.0)))
    return (noise * spread * ramp[None, None, :]).astype(jnp.bfloat16)


def draw_mass_table(key, part):
    key_diag, key_off = jax.random.split(key)
    diagonal = jax.random.uniform(key_diag, (KINDS, ELEM_PTS), jnp.float32, 2.0, 3.0)
    off_part = jax.random.uniform(key_off, (KINDS, ELEM_PTS, ELEM_PTS), jnp.float32, -0.03, 0.03)
    symmetric = 0.5 * (off_part + jnp.swapaxes(off_part, 1, 2))
    position = jnp.arange(ELEM_PTS, dtype=jnp.int32)
    on_diag = position[:, None] == position[None, :]
    return jnp.where(on_diag[None], diagonal[:, :, None], symmetric)


def draw_offsets(key, part):
    key_vals, key_perm = jax.random.split(key)
    values = jax.random.randint(key_vals, (NB,), 0, RECORD - NT + 1, dtype=jnp.int32)
    order = jax.random.permutation(key_perm, NB)
    values = values.at[order[0]].set(0)
    values = values.at[order[1]].set(RECORD - NT)
    return values


def plant(values, rng, least, top_value):
    longest = values.shape.index(max(values.shape))
    spots = []
    for shift in (0, 1):
        where = [jax.random.randint(jax.random.fold_in(rng, axis), (), 0, length) for axis, length in enumerate(values.shape)]
        where[longest] = (where[longest] + shift) % values.shape[longest]
        spots.append(tuple(where))
    return values.at[spots[0]].set(least).at[spots[1]].set(top_value)


def shard_levels(own_key, shape, cuts, smallest, high):
    loudness = 1.0
    for dim, shards_of in cuts:
        draws = jax.random.uniform(jax.random.fold_in(jax.random.fold_in(own_key, 6), dim), (shards_of,), jnp.float32, smallest / len(cuts), high / len(cuts))
        loudness = loudness * jnp.repeat(jnp.exp(draws), shape[dim] // shards_of).reshape((-1,) + (1,) * (len(shape) - 1 - dim))
    return loudness


def centred(rng, extent, scale, reach, cuts=(), held_as=jnp.bfloat16):
    gain = shard_levels(rng, extent, cuts, -0.22, 0.18) if cuts else 1.0
    values = jax.random.normal(rng, extent, jnp.float32) * scale * gain
    return jnp.minimum(jnp.maximum(values, -reach), reach).astype(held_as)


def setup_inputs(seed: int = 0) -> dict:
    key_of = jax.random.split(jax.random.key(seed), 6)
    return {
        "snapshots": draw_snapshots(jax.random.fold_in(key_of[5], 71), 0),
        "basis": centred(key_of[1], (2, F, RANK, NVAR, NPTS), 1.0, 6.0, ((4, 512),)),
        "mass_table": draw_mass_table(jax.random.fold_in(key_of[5], 71), 0),
        "elem_kind": plant(jax.random.randint(key_of[3], (ELEMS,), 0, KINDS), jax.random.fold_in(key_of[3], 1), 0, KINDS - 1).astype(jnp.int32),
        "offsets": draw_offsets(jax.random.fold_in(key_of[5], 71), 0),
    }


def spectral_table(offsets, window_len, freq_count, record_len):
    snap_idx = jnp.arange(record_len, dtype=jnp.int32)
    time_lag = snap_idx[None, :] - offsets[:, None].astype(jnp.int32)
    inside = (time_lag >= 0) & (time_lag < window_len)
    lag_clip = jnp.clip(time_lag, 0, window_len - 1)
    lag_float = lag_clip.astype(jnp.float32)
    hann_wt = 0.5 - 0.5 * jnp.cos(2.0 * math.pi / window_len * lag_float)
    norm_wt = 1.0 / math.sqrt(0.375 * window_len)
    freq_idx = jnp.arange(freq_count, dtype=jnp.int32)
    phase_int = jnp.mod(freq_idx[:, None, None] * lag_clip[None], window_len)
    angle = 2.0 * math.pi / window_len * phase_int.astype(jnp.float32)
    weight = jnp.where(inside, hann_wt * norm_wt, jnp.zeros_like(hann_wt))[None]
    real_part = weight * jnp.cos(angle)
    imag_part = -weight * jnp.sin(angle)
    return jnp.stack([real_part, imag_part]).astype(jnp.bfloat16)

def apply_mass(field, mass_blk):
    lead = field.shape[:-1]
    elem_count = mass_blk.shape[0]
    shaped = field.reshape(lead + (elem_count, ELEM_PTS))
    result = jnp.einsum('...ep,epq->...eq', shaped, mass_blk, precision=lax.Precision.HIGHEST)
    return result.reshape(field.shape)

def project(mode_rows, weighted):
    real_out = jnp.einsum('fkx,fbx->fbk', mode_rows[0], weighted[0]) + jnp.einsum('fkx,fbx->fbk', mode_rows[1], weighted[1])
    imag_out = jnp.einsum('fkx,fbx->fbk', mode_rows[0], weighted[1]) - jnp.einsum('fkx,fbx->fbk', mode_rows[1], weighted[0])
    return jnp.stack([real_out, imag_out])

def time_kernel(dft_table, coeffs):
    table_f = dft_table.astype(jnp.float32)
    coeff_round = lax.optimization_barrier(coeffs.astype(jnp.bfloat16)).astype(jnp.float32)
    real_out = jnp.einsum('fbt,fbk->fkt', table_f[0], coeff_round[0]) - jnp.einsum('fbt,fbk->fkt', table_f[1], coeff_round[1])
    imag_out = jnp.einsum('fbt,fbk->fkt', table_f[0], coeff_round[1]) + jnp.einsum('fbt,fbk->fkt', table_f[1], coeff_round[0])
    return jnp.stack([real_out, imag_out]).astype(jnp.bfloat16)

def reference(snapshots, basis, mass_table, elem_kind, offsets):
    dft_table = spectral_table(offsets, NT, F, RECORD)
    table_flat = dft_table.reshape(2 * F * NB, RECORD)
    entries = NVAR * NPTS
    block_pts = math.gcd(NPTS, 4096)
    block_count = NPTS // block_pts
    block_elems = block_pts // ELEM_PTS
    block_ids = jnp.arange(block_count, dtype=jnp.int32)

    def block_data(block_index):
        first_pt = (block_index * block_pts).astype(jnp.int32)
        record_blk = lax.dynamic_slice_in_dim(snapshots, first_pt, block_pts, 2)
        kinds_blk = lax.dynamic_slice_in_dim(elem_kind, (block_index * block_elems).astype(jnp.int32), block_elems, 0)
        mass_blk = mass_table[kinds_blk]
        return (record_blk.reshape(RECORD, NVAR * block_pts), mass_blk, first_pt)

    def coefficient_part(block_index):
        record_flat, mass_blk, first_pt = block_data(block_index)
        basis_blk = lax.dynamic_slice_in_dim(basis, first_pt, block_pts, 4)
        spectra = jnp.dot(table_flat, record_flat, preferred_element_type=jnp.float32)
        weighted = apply_mass(spectra.reshape(2, F, NB, NVAR, block_pts), mass_blk).astype(jnp.bfloat16)
        weighted = weighted.reshape(2, F, NB, NVAR * block_pts).astype(jnp.float32)
        mode_rows = basis_blk.reshape(2, F, RANK, NVAR * block_pts).astype(jnp.float32)
        return project(mode_rows, weighted)
    coeffs = lax.optimization_barrier(jnp.sum(lax.map(coefficient_part, block_ids), axis=0)) / math.sqrt(entries)
    kernel = time_kernel(dft_table, coeffs).reshape(2 * F * RANK, RECORD)

    def field_block(block_index):
        record_flat, mass_blk, first_pt = block_data(block_index)
        fields = jnp.dot(kernel, record_flat, preferred_element_type=jnp.float32)
        return (fields.reshape(2, F, RANK, NVAR, block_pts), mass_blk)

    def energy_part(block_index):
        fields, mass_blk = field_block(block_index)
        massed = apply_mass(fields, mass_blk)
        return lax.optimization_barrier(jnp.sum(fields * massed, axis=(0, 3, 4)))
    energy = lax.optimization_barrier(jnp.sum(lax.map(energy_part, block_ids), axis=0))
    factor = 1.0 / jnp.sqrt(energy / entries + 1e-06)

    def output_part(block_index):
        fields, mass_blk = field_block(block_index)
        return (fields * factor[None, :, :, None, None]).astype(jnp.bfloat16)
    pieces = lax.map(output_part, block_ids)
    new_basis = jnp.moveaxis(pieces, 0, 4).reshape(2, F, RANK, NVAR, NPTS)
    return (coeffs, new_basis)
```

```python
import functools
import math

import jax
import jax.numpy as jnp
import numpy as np
from jax import lax
from jax.experimental import pallas as pl
from jax.experimental.pallas import tpu as pltpu
from jax.sharding import Mesh
from jax.sharding import PartitionSpec as P

NT = 256
TM = ("tm_0", "tm_1", "tm_2")
SPACE_TM = ("space", "tm_0", "tm_1", "tm_2")
NEAR = ("tm_2", "space")
FAR = ("tm_0", "tm_1")

F = 33
NB = 8
RANK = 16
NVAR = 5
PTS = 128
RECORD = 512
GROUP = 8
GROUPS = 5
ROWS = 544
FLAT = NVAR * PTS
TILES = 16
VMEM_LIMIT = 48 * 1024 * 1024


def window_rows():
    j = np.arange(NT)
    weight = (0.5 - 0.5 * np.cos(2 * np.pi * j / NT)) / math.sqrt(0.375 * NT)
    angle = 2 * np.pi * (np.arange(F)[:, None] * j % NT) / NT
    rows = np.stack([weight * np.cos(angle), -weight * np.sin(angle)], axis=1)
    out = np.zeros((2 * GROUP * GROUPS, RECORD), np.float32)
    out[: 2 * F, :NT] = rows.reshape(2 * F, NT)
    return out


def lanes(shape):
    return lax.broadcasted_iota(jnp.int32, shape, len(shape) - 1)


def prepare(offsets, kinds, rows, mass, table, mass_split, held):
    for b in range(NB):
        moved = pltpu.roll(rows[...], offsets[b], axis=1)
        for q in range(RECORD // 128):
            held[q, pl.ds(b, 2 * GROUP * GROUPS, stride=NB), :] = moved[:, q * 128 : (q + 1) * 128]
    for q in range(RECORD // 128):
        table[:, q * 128 : (q + 1) * 128] = held[q, :ROWS, :].astype(jnp.bfloat16)
    none = jnp.zeros((64, 64), jnp.float32)
    whole = jnp.concatenate(
        [
            jnp.concatenate([mass[kinds[0]], none], axis=1),
            jnp.concatenate([none, mass[kinds[1]]], axis=1),
        ],
        axis=0,
    )
    high = whole.astype(jnp.bfloat16)
    low = (whole - high.astype(jnp.float32)).astype(jnp.bfloat16)
    mass_split[:, :PTS] = high
    mass_split[:, PTS:] = low


def project(record, basis, table, mass_split, spectra, products, weighted, spec_rows):
    spectra[ROWS:, :] = jnp.zeros((GROUPS * 128 - ROWS, FLAT), jnp.bfloat16)
    weighted[ROWS:, :] = jnp.zeros((GROUPS * 128 - ROWS, 2 * FLAT), jnp.bfloat16)
    for lo, hi in ((0, 256), (256, 512), (512, 640)):
        part = jnp.dot(table[...], record[:, lo:hi], preferred_element_type=jnp.float32)
        spectra[:ROWS, lo:hi] = part.astype(jnp.bfloat16)
        pairs = part.reshape(ROWS // 16, 2, 8, hi - lo)
        spec_rows[:, lo:hi] = pairs[:, 0].reshape(ROWS // 2, hi - lo).astype(jnp.bfloat16)
        spec_rows[:, FLAT + lo : FLAT + hi] = (
            pairs[:, 1].reshape(ROWS // 2, hi - lo).astype(jnp.bfloat16)
        )
    for v in range(NVAR):
        at = slice(v * PTS, (v + 1) * PTS)
        to = slice(FLAT + v * PTS, FLAT + (v + 1) * PTS)
        both = jnp.dot(spectra[:ROWS, at], mass_split[...], preferred_element_type=jnp.float32)
        one = both[:, :PTS] + both[:, PTS:]
        weighted[:ROWS, at] = one.astype(jnp.bfloat16)
        pairs = one.reshape(ROWS // 16, 2, 8, PTS)
        turned = jnp.stack([pairs[:, 1], -pairs[:, 0]], axis=1).reshape(ROWS, PTS)
        weighted[:ROWS, to] = turned.astype(jnp.bfloat16)
    across = (((1,), (1,)), ((), ()))
    for g in range(GROUPS):
        count = min(GROUP, F - g * GROUP)
        fs = slice(g * GROUP, g * GROUP + count)
        right = weighted[g * 128 : (g + 1) * 128, :]
        modes = jnp.concatenate(
            [basis[c, fs, v].reshape(count * RANK, PTS) for c in range(2) for v in range(NVAR)],
            axis=1,
        )
        rows = max(count * NB, 16)
        own = spec_rows[g * 64 : g * 64 + rows, :]
        on_modes = lax.dot_general(modes, right, across, preferred_element_type=jnp.float32)
        on_own = lax.dot_general(own, right, across, preferred_element_type=jnp.float32)
        place = lanes((RANK, 128)) // 16
        kept_modes = jnp.zeros((RANK, 128), jnp.float32)
        kept_own = jnp.zeros((NB, 128), jnp.float32)
        for i in range(count):
            kept_modes = jnp.where(place == i, on_modes[i * RANK : (i + 1) * RANK], kept_modes)
            kept_own = jnp.where(place[:NB] == i, on_own[i * NB : (i + 1) * NB], kept_own)
        products[3 * g] = kept_modes[:8]
        products[3 * g + 1] = kept_modes[8:]
        products[3 * g + 2] = kept_own
    products[TILES - 1] = jnp.zeros((8, 128), jnp.float32)


def swapped(value):
    real = lanes(value.shape) // 8 % 2 == 0
    return jnp.where(real, pltpu.roll(value, 120, axis=1), pltpu.roll(value, 8, axis=1))


def signed(value):
    real = lanes(value.shape) // 8 % 2 == 0
    return jnp.where(real, value, -value)


def update(entries, totals, spectra, coeffs, out, staged, sems):
    exact = functools.partial(
        jnp.dot, preferred_element_type=jnp.float32, precision=lax.Precision.HIGHEST
    )
    place = lanes((RANK, 128)) // 16
    row_place = lax.broadcasted_iota(jnp.int32, (128, 128), 0) // 16
    same = (row_place == lanes((128, 128)) // 16).astype(jnp.float32)
    copies = []
    for g in range(GROUPS):
        count = min(GROUP, F - g * GROUP)
        coeff = jnp.concatenate([totals[3 * g], totals[3 * g + 1]], axis=0)
        coeff = coeff * (1.0 / math.sqrt(entries))
        coeffs[g] = coeff
        coeff = coeff.astype(jnp.bfloat16).astype(jnp.float32)
        gram = totals[3 * g + 2]
        first, second = signed(gram), swapped(gram)
        tiles = []
        for i in range(GROUP):
            tiles += [
                jnp.where(place[:8] == i, first, 0.0),
                jnp.where(place[:8] == i, second, 0.0),
            ]
        applied = exact(coeff, jnp.concatenate(tiles, axis=0))
        energy = exact(coeff * applied, same)
        factor = 1.0 / jnp.sqrt(jnp.maximum(energy, 0.0) / entries + 1e-06)
        scaled = coeff * factor
        real, imag = signed(scaled), swapped(scaled)
        left = []
        for i in range(count):
            left += [jnp.where(place == i, real, 0.0), jnp.where(place == i, imag, 0.0)]
        left = jnp.concatenate(left, axis=0).astype(jnp.bfloat16)
        fields = jnp.dot(
            left, spectra[g * 128 : (g + 1) * 128, :], preferred_element_type=jnp.float32
        ).astype(jnp.bfloat16)
        for i in range(count):
            for c in range(2):
                row = (2 * i + c) * RANK
                for v in range(NVAR):
                    staged[c, g * GROUP + i, v] = fields[
                        row : row + RANK, v * PTS : (v + 1) * PTS
                    ]
        for c in range(2):
            fs = pl.ds(g * GROUP, count)
            copy = pltpu.make_async_copy(staged.at[c, fs], out.at[c, fs], sems.at[2 * g + c])
            copy.start()
            copies.append(copy)
    for copy in copies:
        copy.wait()


def in_vmem(count):
    return [pl.BlockSpec(memory_space=pltpu.VMEM)] * count


def in_smem(count):
    return [pl.BlockSpec(memory_space=pltpu.SMEM)] * count


def params():
    return pltpu.CompilerParams(vmem_limit_bytes=VMEM_LIMIT)


def prepared(offsets, kinds, mass):
    return pl.pallas_call(
        prepare,
        out_shape=(
            jax.ShapeDtypeStruct((ROWS, RECORD), jnp.bfloat16),
            jax.ShapeDtypeStruct((PTS, 2 * PTS), jnp.bfloat16),
        ),
        in_specs=in_smem(2) + in_vmem(2),
        out_specs=tuple(in_vmem(2)),
        scratch_shapes=[pltpu.VMEM((RECORD // 128, 2 * NB * GROUP * GROUPS, 128), jnp.float32)],
        compiler_params=params(),
        name="tables",
    )(offsets, kinds, jnp.asarray(window_rows()), mass)


def projected(record, basis, table, mass_split):
    return pl.pallas_call(
        project,
        out_shape=(
            jax.ShapeDtypeStruct((GROUPS * 128, FLAT), jnp.bfloat16),
            jax.ShapeDtypeStruct((TILES, 8, 128), jnp.float32),
        ),
        in_specs=in_vmem(4),
        out_specs=tuple(in_vmem(2)),
        scratch_shapes=[
            pltpu.VMEM((GROUPS * 128, 2 * FLAT), jnp.bfloat16),
            pltpu.VMEM((ROWS // 2, 2 * FLAT), jnp.bfloat16),
        ],
        compiler_params=params(),
        name="spectra_products",
    )(record, basis, table, mass_split)


def updated(entries, totals, spectra):
    shape = (2, F, NVAR, RANK, PTS)
    return pl.pallas_call(
        functools.partial(update, entries),
        out_shape=(
            jax.ShapeDtypeStruct((GROUPS, RANK, 128), jnp.float32),
            jax.ShapeDtypeStruct(shape, jnp.bfloat16),
        ),
        in_specs=in_vmem(2),
        out_specs=(pl.BlockSpec(memory_space=pltpu.VMEM), pl.BlockSpec(memory_space=pl.ANY)),
        scratch_shapes=[
            pltpu.VMEM(shape, jnp.bfloat16),
            pltpu.SemaphoreType.DMA((2 * GROUPS,)),
        ],
        compiler_params=params(),
        name="fields_update",
    )(totals, spectra)


def exchanged(parts, axes):
    return lax.all_to_all(parts, axes, split_axis=0, concat_axis=0, tiled=True)


def sent_to_all(value, axes):
    size = math.prod(lax.axis_size(a) for a in axes)
    return exchanged(jnp.broadcast_to(value[None], (size, *value.shape)), axes)


def on_device(snapshots, basis, mass_table, elem_kind, offsets):
    parts = snapshots.transpose(1, 0, 2).reshape(NVAR, 8, 64, PTS).transpose(2, 0, 1, 3)
    arrived = exchanged(parts, TM)
    record = arrived.transpose(0, 2, 1, 3).reshape(RECORD, FLAT)
    table, mass_split = prepared(offsets, elem_kind, mass_table)
    spectra, products = projected(record, basis.transpose(0, 1, 3, 2, 4), table, mass_split)
    own = exchanged(products, NEAR).sum(axis=0)
    own = sent_to_all(own, FAR).sum(axis=0)
    totals = sent_to_all(own, NEAR)
    entries = FLAT * lax.axis_size(TM) * lax.axis_size("space")
    tiles, new_basis = updated(entries, totals, spectra)
    coeffs = tiles.reshape(GROUPS, RANK, GROUP, 2, NB).transpose(3, 0, 2, 4, 1)
    coeffs = coeffs.reshape(2, GROUPS * GROUP, NB, RANK)[:, :F]
    return (coeffs, new_basis.transpose(0, 1, 3, 2, 4))


def solution(mesh):
    finer = Mesh(
        mesh.devices.reshape(4, 8, 2, mesh.shape["space"]), ("tm_0", "tm_1", "tm_2", "space")
    )
    return jax.shard_map(
        on_device,
        mesh=finer,
        in_specs=(P(TM, None, "space"), P(None, None, None, None, SPACE_TM), P(), P(SPACE_TM), P()),
        out_specs=(P(), P(None, None, None, None, SPACE_TM)),
        check_vma=False,
    )
```

```python
import functools
import math

import jax
import jax.numpy as jnp
import numpy as np
from jax import lax
from jax.experimental import pallas as pl
from jax.experimental.pallas import tpu as pltpu
from jax.sharding import Mesh
from jax.sharding import PartitionSpec as P

NT = 256
TM = ("tm_0", "tm_1", "tm_2")
SPACE_TM = ("space", "tm_0", "tm_1", "tm_2")
NEAR = ("tm_2", "space")
FAR = ("tm_0", "tm_1")

F = 33
NB = 8
RANK = 16
NVAR = 5
PTS = 128
RECORD = 512
GROUP = 8
GROUPS = 5
ROWS = 544
FLAT = NVAR * PTS
TILES = 16


def window_rows():
    j = np.arange(NT)
    weight = (0.5 - 0.5 * np.cos(2 * np.pi * j / NT)) / math.sqrt(0.375 * NT)
    angle = 2 * np.pi * (np.arange(F)[:, None] * j % NT) / NT
    rows = np.stack([weight * np.cos(angle), -weight * np.sin(angle)], axis=1)
    out = np.zeros((2 * GROUP * GROUPS, RECORD), np.float32)
    out[: 2 * F, :NT] = rows.reshape(2 * F, NT)
    return out


def lanes(shape):
    return lax.broadcasted_iota(jnp.int32, shape, len(shape) - 1)


def spread(snapshots, parts, sems):
    copies = []
    for v in range(NVAR):
        copy = pltpu.make_async_copy(snapshots.at[v], parts.at[:, v], sems.at[v])
        copy.start()
        copies.append(copy)
    for copy in copies:
        copy.wait()


def halves(value):
    high = value.astype(jnp.bfloat16)
    return high, (value - high.astype(jnp.float32)).astype(jnp.bfloat16)


def prepare(offsets, kinds, rows, mass, table, mass_split, held):
    for b in range(NB):
        moved = pltpu.roll(rows[...], offsets[b], axis=1)
        for q in range(RECORD // 128):
            held[q, pl.ds(b, 2 * GROUP * GROUPS, stride=NB), :] = moved[:, q * 128 : (q + 1) * 128]
    for q in range(RECORD // 128):
        table[:, q * 128 : (q + 1) * 128] = held[q, :ROWS, :].astype(jnp.bfloat16)
    none = jnp.zeros((64, 64), jnp.float32)
    whole = jnp.concatenate(
        [
            jnp.concatenate([mass[kinds[0]], none], axis=1),
            jnp.concatenate([none, mass[kinds[1]]], axis=1),
        ],
        axis=0,
    )
    high, low = halves(whole)
    for at in (0, PTS):
        mass_split[at : at + PTS, :PTS] = high
        mass_split[at : at + PTS, PTS:] = low


def project(record, basis, table, mass_split, high_part, low_part, products, weighted, spec_rows):
    high_part[ROWS:, :] = jnp.zeros((GROUPS * 128 - ROWS, FLAT), jnp.bfloat16)
    low_part[ROWS:, :] = jnp.zeros((GROUPS * 128 - ROWS, FLAT), jnp.bfloat16)
    weighted[ROWS:, :] = jnp.zeros((GROUPS * 128 - ROWS, 2 * FLAT), jnp.bfloat16)
    for lo, hi in ((0, 256), (256, 512), (512, 640)):
        part = jnp.dot(table[...], record[:, lo:hi], preferred_element_type=jnp.float32)
        high_part[:ROWS, lo:hi], low_part[:ROWS, lo:hi] = halves(part)
        pairs = part.reshape(ROWS // 16, 2, 8, hi - lo)
        spec_rows[:, lo:hi] = pairs[:, 0].reshape(ROWS // 2, hi - lo).astype(jnp.bfloat16)
        spec_rows[:, FLAT + lo : FLAT + hi] = (
            pairs[:, 1].reshape(ROWS // 2, hi - lo).astype(jnp.bfloat16)
        )
    for v in range(NVAR):
        at = slice(v * PTS, (v + 1) * PTS)
        to = slice(FLAT + v * PTS, FLAT + (v + 1) * PTS)
        both = jnp.concatenate([high_part[:ROWS, at], low_part[:ROWS, at]], axis=1)
        both = jnp.dot(both, mass_split[...], preferred_element_type=jnp.float32)
        one = both[:, :PTS] + both[:, PTS:]
        weighted[:ROWS, at] = one.astype(jnp.bfloat16)
        pairs = one.reshape(ROWS // 16, 2, 8, PTS)
        turned = jnp.stack([pairs[:, 1], -pairs[:, 0]], axis=1).reshape(ROWS, PTS)
        weighted[:ROWS, to] = turned.astype(jnp.bfloat16)
    across = (((1,), (1,)), ((), ()))
    place = lanes((RANK, 128)) // 16
    for g in range(GROUPS):
        count = min(GROUP, F - g * GROUP)
        fs = slice(g * GROUP, g * GROUP + count)
        right = weighted[g * 128 : (g + 1) * 128, :]
        modes = jnp.concatenate(
            [basis[c, fs, v].reshape(count * RANK, PTS) for c in range(2) for v in range(NVAR)],
            axis=1,
        )
        rows = max(count * NB, 16)
        own = spec_rows[g * 64 : g * 64 + rows, :]
        on_modes = lax.dot_general(modes, right, across, preferred_element_type=jnp.float32)
        on_own = lax.dot_general(own, right, across, preferred_element_type=jnp.float32)
        kept_modes = jnp.zeros((RANK, 128), jnp.float32)
        kept_own = jnp.zeros((NB, 128), jnp.float32)
        for i in range(count):
            kept_modes = jnp.where(place == i, on_modes[i * RANK : (i + 1) * RANK], kept_modes)
            kept_own = jnp.where(place[:NB] == i, on_own[i * NB : (i + 1) * NB], kept_own)
        products[3 * g] = kept_modes[:8]
        products[3 * g + 1] = kept_modes[8:]
        products[3 * g + 2] = kept_own
    products[TILES - 1] = jnp.zeros((8, 128), jnp.float32)


def swapped(value):
    real = lanes(value.shape) // 8 % 2 == 0
    return jnp.where(real, pltpu.roll(value, 120, axis=1), pltpu.roll(value, 8, axis=1))


def signed(value):
    real = lanes(value.shape) // 8 % 2 == 0
    return jnp.where(real, value, -value)


def update(entries, totals, high_part, low_part, coeffs, out, ordered, staged, sems):
    place = lanes((RANK, 128)) // 16
    row_place = lax.broadcasted_iota(jnp.int32, (256, 128), 0) // 16 % 8
    same = (row_place == lanes((256, 128)) // 16).astype(jnp.bfloat16)
    exact, rounded, terms = [], [], []
    for g in range(GROUPS):
        coeff = jnp.concatenate([totals[3 * g], totals[3 * g + 1]], axis=0)
        coeff = coeff * (1.0 / math.sqrt(entries))
        exact.append(coeff)
        short = coeff.astype(jnp.bfloat16)
        coeff = short.astype(jnp.float32)
        rounded.append(coeff)
        gram = totals[3 * g + 2]
        first, second = signed(gram), swapped(gram)
        tiles = []
        for i in range(GROUP):
            tiles += [
                jnp.where(place[:8] == i, first, 0.0),
                jnp.where(place[:8] == i, second, 0.0),
            ]
        pair = jnp.concatenate(halves(jnp.concatenate(tiles, axis=0)), axis=0)
        applied = jnp.dot(
            jnp.concatenate([short, short], axis=1), pair, preferred_element_type=jnp.float32
        )
        terms.append(coeff * applied)
    terms = jnp.concatenate(halves(jnp.concatenate(terms, axis=0)), axis=1)
    energy = jnp.dot(terms, same, preferred_element_type=jnp.float32)
    factor = 1.0 / jnp.sqrt(jnp.maximum(energy, 0.0) / entries + 1e-06)
    copies = []
    for g in range(GROUPS):
        count = min(GROUP, F - g * GROUP)
        real, imag = signed(rounded[g]), swapped(rounded[g])
        left = []
        for i in range(count):
            left += [jnp.where(place == i, real, 0.0), jnp.where(place == i, imag, 0.0)]
        left = jnp.concatenate(left, axis=0).astype(jnp.bfloat16)
        left = jnp.concatenate([left, left], axis=1)
        rows = slice(g * 128, (g + 1) * 128)
        right = jnp.concatenate([high_part[rows, :], low_part[rows, :]], axis=0)
        fields = jnp.dot(left, right, preferred_element_type=jnp.float32)
        for i in range(count):
            scale = factor[g * RANK : (g + 1) * RANK, i * 16 : i * 16 + 1]
            scale = jnp.broadcast_to(scale, (RANK, PTS))
            for c in range(2):
                row = (2 * i + c) * RANK
                for v in range(NVAR):
                    one = fields[row : row + RANK, v * PTS : (v + 1) * PTS] * scale
                    staged[c, g * GROUP + i, v] = one.astype(jnp.bfloat16)
        for c in range(2):
            fs = pl.ds(g * GROUP, count)
            copy = pltpu.make_async_copy(staged.at[c, fs], out.at[c, fs], sems.at[2 * g + c])
            copy.start()
            copies.append(copy)
    lane = lanes((8, 128))
    for c in range(2):
        for b in range(NB):
            index = lane % 8 * 16 + c * 8 + b
            for half in range(2):
                line = jnp.zeros((8, 128), jnp.float32)
                for g in range(GROUPS):
                    moved = jnp.take_along_axis(
                        exact[g][half * 8 : half * 8 + 8], index, axis=1, mode="promise_in_bounds"
                    )
                    line = jnp.where(lane // 8 == g, moved, line)
                ordered[c, b, half * 8 : half * 8 + 8, :] = line[:, :F]
    copy = pltpu.make_async_copy(ordered, coeffs, sems.at[2 * GROUPS])
    copy.start()
    copies.append(copy)
    for copy in copies:
        copy.wait()


def in_vmem(count):
    return [pl.BlockSpec(memory_space=pltpu.VMEM)] * count


def in_smem(count):
    return [pl.BlockSpec(memory_space=pltpu.SMEM)] * count


def params(mib):
    return pltpu.CompilerParams(vmem_limit_bytes=mib * 1024 * 1024)


def anywhere(count):
    return [pl.BlockSpec(memory_space=pl.ANY)] * count


def sent(snapshots):
    return pl.pallas_call(
        spread,
        out_shape=jax.ShapeDtypeStruct((64, NVAR, 8, PTS), jnp.bfloat16),
        in_specs=anywhere(1),
        out_specs=anywhere(1)[0],
        scratch_shapes=[pltpu.SemaphoreType.DMA((NVAR,))],
        compiler_params=params(2),
        name="send_order",
    )(snapshots)


def prepared(offsets, kinds, mass):
    return pl.pallas_call(
        prepare,
        out_shape=(
            jax.ShapeDtypeStruct((ROWS, RECORD), jnp.bfloat16),
            jax.ShapeDtypeStruct((2 * PTS, 2 * PTS), jnp.bfloat16),
        ),
        in_specs=in_smem(2) + in_vmem(2),
        out_specs=tuple(in_vmem(2)),
        scratch_shapes=[
            pltpu.VMEM((RECORD // 128, 2 * NB * GROUP * GROUPS, 128), jnp.float32)
        ],
        compiler_params=params(12),
        name="tables",
    )(offsets, kinds, jnp.asarray(window_rows()), mass)


def projected(record, basis, table, mass_split):
    return pl.pallas_call(
        project,
        out_shape=(
            jax.ShapeDtypeStruct((GROUPS * 128, FLAT), jnp.bfloat16),
            jax.ShapeDtypeStruct((GROUPS * 128, FLAT), jnp.bfloat16),
            jax.ShapeDtypeStruct((TILES, 8, 128), jnp.float32),
        ),
        in_specs=in_vmem(4),
        out_specs=tuple(in_vmem(3)),
        scratch_shapes=[
            pltpu.VMEM((GROUPS * 128, 2 * FLAT), jnp.bfloat16),
            pltpu.VMEM((ROWS // 2, 2 * FLAT), jnp.bfloat16),
        ],
        compiler_params=params(20),
        name="spectra_products",
    )(record, basis, table, mass_split)


def updated(entries, totals, high_part, low_part):
    shape = (2, F, NVAR, RANK, PTS)
    line = (2, NB, RANK, F)
    return pl.pallas_call(
        functools.partial(update, entries),
        out_shape=(
            jax.ShapeDtypeStruct(line, jnp.float32),
            jax.ShapeDtypeStruct(shape, jnp.bfloat16),
        ),
        in_specs=in_vmem(3),
        out_specs=tuple(anywhere(2)),
        scratch_shapes=[
            pltpu.VMEM(line, jnp.float32),
            pltpu.VMEM(shape, jnp.bfloat16),
            pltpu.SemaphoreType.DMA((2 * GROUPS + 1,)),
        ],
        compiler_params=params(20),
        name="fields_update",
    )(totals, high_part, low_part)


def exchanged(parts, axes):
    return lax.all_to_all(parts, axes, split_axis=0, concat_axis=0, tiled=True)


def sent_to_all(value, axes):
    size = math.prod(lax.axis_size(a) for a in axes)
    return exchanged(jnp.broadcast_to(value[None], (size, *value.shape)), axes)


def on_device(snapshots, basis, mass_table, elem_kind, offsets):
    lines = snapshots.transpose(1, 0, 2).reshape(NVAR, 8, 64, PTS).transpose(0, 2, 1, 3)
    arrived = exchanged(sent(lines), TM)
    record = arrived.transpose(0, 2, 1, 3).reshape(RECORD, FLAT)
    table, mass_split = prepared(offsets, elem_kind, mass_table)
    high_part, low_part, products = projected(
        record, basis.transpose(0, 1, 3, 2, 4), table, mass_split
    )
    own = exchanged(products, NEAR).sum(axis=0)
    own = sent_to_all(own, FAR).sum(axis=0)
    totals = sent_to_all(own, NEAR)
    entries = FLAT * lax.axis_size(TM) * lax.axis_size("space")
    coeffs, new_basis = updated(entries, totals, high_part, low_part)
    return (coeffs.transpose(0, 3, 1, 2), new_basis.transpose(0, 1, 3, 2, 4))


def solution(mesh):
    finer = Mesh(
        mesh.devices.reshape(4, 8, 2, mesh.shape["space"]), ("tm_0", "tm_1", "tm_2", "space")
    )
    return jax.shard_map(
        on_device,
        mesh=finer,
        in_specs=(P(TM, None, "space"), P(None, None, None, None, SPACE_TM), P(), P(SPACE_TM), P()),
        out_specs=(P(), P(None, None, None, None, SPACE_TM)),
        check_vma=False,
    )
```

```python
import functools
import math

import jax
import jax.numpy as jnp
import numpy as np
from jax import lax
from jax.experimental import pallas as pl
from jax.experimental.pallas import tpu as pltpu
from jax.sharding import Mesh
from jax.sharding import PartitionSpec as P

NT = 256
TM = ("tm_0", "tm_1", "tm_2")
SPACE_TM = ("space", "tm_0", "tm_1", "tm_2")
NEAR = ("tm_2", "space")
FAR = ("tm_0", "tm_1")

F = 33
NB = 8
RANK = 16
NVAR = 5
PTS = 128
RECORD = 512
GROUP = 8
GROUPS = 5
ROWS = 544
FLAT = NVAR * PTS
TILES = 16


def window_rows():
    j = np.arange(NT)
    weight = (0.5 - 0.5 * np.cos(2 * np.pi * j / NT)) / math.sqrt(0.375 * NT)
    angle = 2 * np.pi * (np.arange(F)[:, None] * j % NT) / NT
    rows = np.stack([weight * np.cos(angle), -weight * np.sin(angle)], axis=1)
    out = np.zeros((2 * GROUP * GROUPS, RECORD), np.float32)
    out[: 2 * F, :NT] = rows.reshape(2 * F, NT)
    return out


def lanes(shape):
    return lax.broadcasted_iota(jnp.int32, shape, len(shape) - 1)


def spread(snapshots, parts, sems):
    copies = []
    for v in range(NVAR):
        copy = pltpu.make_async_copy(snapshots.at[v], parts.at[:, v], sems.at[v])
        copy.start()
        copies.append(copy)
    for copy in copies:
        copy.wait()


def halves(value):
    high = value.astype(jnp.bfloat16)
    return high, (value - high.astype(jnp.float32)).astype(jnp.bfloat16)


def prepare(offsets, kinds, rows, mass, table, mass_split, held):
    for b in range(NB):
        moved = pltpu.roll(rows[...], offsets[b], axis=1)
        for q in range(RECORD // 128):
            held[q, pl.ds(b, 2 * GROUP * GROUPS, stride=NB), :] = moved[:, q * 128 : (q + 1) * 128]
    for q in range(RECORD // 128):
        table[:, q * 128 : (q + 1) * 128] = held[q, :ROWS, :].astype(jnp.bfloat16)
    none = jnp.zeros((64, 64), jnp.float32)
    whole = jnp.concatenate(
        [
            jnp.concatenate([mass[kinds[0]], none], axis=1),
            jnp.concatenate([none, mass[kinds[1]]], axis=1),
        ],
        axis=0,
    )
    high, low = halves(whole)
    for at in (0, PTS):
        mass_split[at : at + PTS, :PTS] = high
        mass_split[at : at + PTS, PTS:] = low


def project(record, basis, table, mass_split, spectra, products, low_part, weighted, spec_rows):
    spectra[ROWS:, :] = jnp.zeros((GROUPS * 128 - ROWS, FLAT), jnp.bfloat16)
    weighted[ROWS:, :] = jnp.zeros((GROUPS * 128 - ROWS, 2 * FLAT), jnp.bfloat16)
    for lo, hi in ((0, 256), (256, 512), (512, 640)):
        part = jnp.dot(table[...], record[:, lo:hi], preferred_element_type=jnp.float32)
        spectra[:ROWS, lo:hi], low_part[:, lo:hi] = halves(part)
        pairs = part.reshape(ROWS // 16, 2, 8, hi - lo)
        spec_rows[:, lo:hi] = pairs[:, 0].reshape(ROWS // 2, hi - lo).astype(jnp.bfloat16)
        spec_rows[:, FLAT + lo : FLAT + hi] = (
            pairs[:, 1].reshape(ROWS // 2, hi - lo).astype(jnp.bfloat16)
        )
    for v in range(NVAR):
        at = slice(v * PTS, (v + 1) * PTS)
        to = slice(FLAT + v * PTS, FLAT + (v + 1) * PTS)
        both = jnp.concatenate([spectra[:ROWS, at], low_part[:, at]], axis=1)
        both = jnp.dot(both, mass_split[...], preferred_element_type=jnp.float32)
        one = both[:, :PTS] + both[:, PTS:]
        weighted[:ROWS, at] = one.astype(jnp.bfloat16)
        pairs = one.reshape(ROWS // 16, 2, 8, PTS)
        turned = jnp.stack([pairs[:, 1], -pairs[:, 0]], axis=1).reshape(ROWS, PTS)
        weighted[:ROWS, to] = turned.astype(jnp.bfloat16)
    across = (((1,), (1,)), ((), ()))
    place = lanes((RANK, 128)) // 16
    for g in range(GROUPS):
        count = min(GROUP, F - g * GROUP)
        fs = slice(g * GROUP, g * GROUP + count)
        right = weighted[g * 128 : (g + 1) * 128, :]
        modes = jnp.concatenate(
            [basis[c, fs, v].reshape(count * RANK, PTS) for c in range(2) for v in range(NVAR)],
            axis=1,
        )
        rows = max(count * NB, 16)
        own = spec_rows[g * 64 : g * 64 + rows, :]
        on_modes = lax.dot_general(modes, right, across, preferred_element_type=jnp.float32)
        on_own = lax.dot_general(own, right, across, preferred_element_type=jnp.float32)
        kept_modes = jnp.zeros((RANK, 128), jnp.float32)
        kept_own = jnp.zeros((NB, 128), jnp.float32)
        for i in range(count):
            kept_modes = jnp.where(place == i, on_modes[i * RANK : (i + 1) * RANK], kept_modes)
            kept_own = jnp.where(place[:NB] == i, on_own[i * NB : (i + 1) * NB], kept_own)
        products[3 * g] = kept_modes[:8]
        products[3 * g + 1] = kept_modes[8:]
        products[3 * g + 2] = kept_own
    products[TILES - 1] = jnp.zeros((8, 128), jnp.float32)


def swapped(value):
    real = lanes(value.shape) // 8 % 2 == 0
    return jnp.where(real, pltpu.roll(value, 120, axis=1), pltpu.roll(value, 8, axis=1))


def signed(value):
    real = lanes(value.shape) // 8 % 2 == 0
    return jnp.where(real, value, -value)


def update(entries, totals, spectra, coeffs, out, ordered, staged, sems):
    place = lanes((RANK, 128)) // 16
    row_place = lax.broadcasted_iota(jnp.int32, (256, 128), 0) // 16 % 8
    same = (row_place == lanes((256, 128)) // 16).astype(jnp.bfloat16)
    exact, rounded, terms = [], [], []
    for g in range(GROUPS):
        coeff = jnp.concatenate([totals[3 * g], totals[3 * g + 1]], axis=0)
        coeff = coeff * (1.0 / math.sqrt(entries))
        exact.append(coeff)
        short = coeff.astype(jnp.bfloat16)
        coeff = short.astype(jnp.float32)
        rounded.append(coeff)
        gram = totals[3 * g + 2]
        first, second = signed(gram), swapped(gram)
        tiles = []
        for i in range(GROUP):
            tiles += [
                jnp.where(place[:8] == i, first, 0.0),
                jnp.where(place[:8] == i, second, 0.0),
            ]
        pair = jnp.concatenate(halves(jnp.concatenate(tiles, axis=0)), axis=0)
        applied = jnp.dot(
            jnp.concatenate([short, short], axis=1), pair, preferred_element_type=jnp.float32
        )
        terms.append(coeff * applied)
    terms = jnp.concatenate(halves(jnp.concatenate(terms, axis=0)), axis=1)
    energy = jnp.dot(terms, same, preferred_element_type=jnp.float32)
    factor = 1.0 / jnp.sqrt(jnp.maximum(energy, 0.0) / entries + 1e-06)
    copies = []
    for g in range(GROUPS):
        count = min(GROUP, F - g * GROUP)
        real, imag = signed(rounded[g]), swapped(rounded[g])
        left = []
        for i in range(count):
            left += [jnp.where(place == i, real, 0.0), jnp.where(place == i, imag, 0.0)]
        left = jnp.concatenate(left, axis=0).astype(jnp.bfloat16)
        right = spectra[g * 128 : (g + 1) * 128, :]
        fields = jnp.dot(left, right, preferred_element_type=jnp.float32)
        for i in range(count):
            scale = factor[g * RANK : (g + 1) * RANK, i * 16 : i * 16 + 1]
            scale = jnp.broadcast_to(scale, (RANK, PTS))
            for c in range(2):
                row = (2 * i + c) * RANK
                for v in range(NVAR):
                    one = fields[row : row + RANK, v * PTS : (v + 1) * PTS] * scale
                    staged[c, g * GROUP + i, v] = one.astype(jnp.bfloat16)
        for c in range(2):
            fs = pl.ds(g * GROUP, count)
            copy = pltpu.make_async_copy(staged.at[c, fs], out.at[c, fs], sems.at[2 * g + c])
            copy.start()
            copies.append(copy)
    lane = lanes((8, 128))
    for c in range(2):
        for b in range(NB):
            index = lane % 8 * 16 + c * 8 + b
            for half in range(2):
                line = jnp.zeros((8, 128), jnp.float32)
                for g in range(GROUPS):
                    moved = jnp.take_along_axis(
                        exact[g][half * 8 : half * 8 + 8], index, axis=1, mode="promise_in_bounds"
                    )
                    line = jnp.where(lane // 8 == g, moved, line)
                ordered[c, b, half * 8 : half * 8 + 8, :] = line[:, :F]
    copy = pltpu.make_async_copy(ordered, coeffs, sems.at[2 * GROUPS])
    copy.start()
    copies.append(copy)
    for copy in copies:
        copy.wait()


def in_vmem(count):
    return [pl.BlockSpec(memory_space=pltpu.VMEM)] * count


def in_smem(count):
    return [pl.BlockSpec(memory_space=pltpu.SMEM)] * count


def params(mib):
    return pltpu.CompilerParams(vmem_limit_bytes=mib * 1024 * 1024)


def anywhere(count):
    return [pl.BlockSpec(memory_space=pl.ANY)] * count


def sent(snapshots):
    return pl.pallas_call(
        spread,
        out_shape=jax.ShapeDtypeStruct((64, NVAR, 8, PTS), jnp.bfloat16),
        in_specs=[pl.BlockSpec(memory_space=pltpu.HBM)],
        out_specs=anywhere(1)[0],
        scratch_shapes=[pltpu.SemaphoreType.DMA((NVAR,))],
        compiler_params=params(2),
        name="send_order",
    )(pltpu.with_memory_space_constraint(snapshots, pltpu.HBM))


def prepared(offsets, kinds, mass):
    return pl.pallas_call(
        prepare,
        out_shape=(
            jax.ShapeDtypeStruct((ROWS, RECORD), jnp.bfloat16),
            jax.ShapeDtypeStruct((2 * PTS, 2 * PTS), jnp.bfloat16),
        ),
        in_specs=in_smem(2) + in_vmem(2),
        out_specs=tuple(in_vmem(2)),
        scratch_shapes=[
            pltpu.VMEM((RECORD // 128, 2 * NB * GROUP * GROUPS, 128), jnp.float32)
        ],
        compiler_params=params(12),
        name="tables",
    )(offsets, kinds, jnp.asarray(window_rows()), mass)


def projected(record, basis, table, mass_split):
    return pl.pallas_call(
        project,
        out_shape=(
            jax.ShapeDtypeStruct((GROUPS * 128, FLAT), jnp.bfloat16),
            jax.ShapeDtypeStruct((TILES, 8, 128), jnp.float32),
        ),
        in_specs=in_vmem(4),
        out_specs=tuple(in_vmem(2)),
        scratch_shapes=[
            pltpu.VMEM((ROWS, FLAT), jnp.bfloat16),
            pltpu.VMEM((GROUPS * 128, 2 * FLAT), jnp.bfloat16),
            pltpu.VMEM((ROWS // 2, 2 * FLAT), jnp.bfloat16),
        ],
        compiler_params=params(20),
        name="spectra_products",
    )(record, basis, table, mass_split)


def updated(entries, totals, spectra):
    shape = (2, F, NVAR, RANK, PTS)
    line = (2, NB, RANK, F)
    return pl.pallas_call(
        functools.partial(update, entries),
        out_shape=(
            jax.ShapeDtypeStruct(line, jnp.float32),
            jax.ShapeDtypeStruct(shape, jnp.bfloat16),
        ),
        in_specs=in_vmem(2),
        out_specs=tuple(anywhere(2)),
        scratch_shapes=[
            pltpu.VMEM(line, jnp.float32),
            pltpu.VMEM(shape, jnp.bfloat16),
            pltpu.SemaphoreType.DMA((2 * GROUPS + 1,)),
        ],
        compiler_params=params(20),
        name="fields_update",
    )(totals, spectra)


def exchanged(parts, axes):
    return lax.all_to_all(parts, axes, split_axis=0, concat_axis=0, tiled=True)


def sent_to_all(value, axes):
    size = math.prod(lax.axis_size(a) for a in axes)
    return exchanged(jnp.broadcast_to(value[None], (size, *value.shape)), axes)


def on_device(snapshots, basis, mass_table, elem_kind, offsets):
    lines = snapshots.transpose(1, 0, 2).reshape(NVAR, 8, 64, PTS).transpose(0, 2, 1, 3)
    arrived = exchanged(sent(lines), TM)
    record = arrived.transpose(0, 2, 1, 3).reshape(RECORD, FLAT)
    table, mass_split = prepared(offsets, elem_kind, mass_table)
    spectra, products = projected(record, basis.transpose(0, 1, 3, 2, 4), table, mass_split)
    own = exchanged(products, NEAR).sum(axis=0)
    own = sent_to_all(own, FAR).sum(axis=0)
    totals = sent_to_all(own, NEAR)
    entries = FLAT * lax.axis_size(TM) * lax.axis_size("space")
    coeffs, new_basis = updated(entries, totals, spectra)
    return (coeffs.transpose(0, 3, 1, 2), new_basis.transpose(0, 1, 3, 2, 4))


def solution(mesh):
    finer = Mesh(
        mesh.devices.reshape(4, 8, 2, mesh.shape["space"]), ("tm_0", "tm_1", "tm_2", "space")
    )
    return jax.shard_map(
        on_device,
        mesh=finer,
        in_specs=(P(TM, None, "space"), P(None, None, None, None, SPACE_TM), P(), P(SPACE_TM), P()),
        out_specs=(P(), P(None, None, None, None, SPACE_TM)),
        check_vma=False,
    )
```

```python
import functools
import math

import jax
import jax.numpy as jnp
import numpy as np
from jax import lax
from jax.experimental import pallas as pl
from jax.experimental.pallas import tpu as pltpu
from jax.sharding import Mesh
from jax.sharding import PartitionSpec as P

NT = 256
TM = ("tm_0", "tm_1", "tm_2")
SPACE_TM = ("space", "tm_0", "tm_1", "tm_2")
NEAR = ("tm_2", "tm_0")
FAR = ("tm_1", "space")

F = 33
NB = 8
RANK = 16
NVAR = 5
PTS = 128
RECORD = 512
GROUP = 8
GROUPS = 5
ROWS = 544
FLAT = NVAR * PTS
SHARE = (8, 3, 4, 128)


def window_rows():
    j = np.arange(NT)
    weight = (0.5 - 0.5 * np.cos(2 * np.pi * j / NT)) / math.sqrt(0.375 * NT)
    angle = 2 * np.pi * (np.arange(F)[:, None] * j % NT) / NT
    rows = np.stack([weight * np.cos(angle), -weight * np.sin(angle)], axis=1)
    out = np.zeros((2 * GROUP * GROUPS, RECORD), np.float32)
    out[: 2 * F, :NT] = rows.reshape(2 * F, NT)
    return out


def lanes(shape):
    return lax.broadcasted_iota(jnp.int32, shape, len(shape) - 1)


def spread(snapshots, parts, sems):
    copies = []
    for v in range(NVAR):
        copy = pltpu.make_async_copy(snapshots.at[v], parts.at[:, v], sems.at[v])
        copy.start()
        copies.append(copy)
    for copy in copies:
        copy.wait()


def halves(value):
    high = value.astype(jnp.bfloat16)
    return high, (value - high.astype(jnp.float32)).astype(jnp.bfloat16)


def part_of(shape, size):
    return lanes(shape) // size


def put(products, tile, value):
    for half in range(2):
        at = 2 * tile + half
        products[at // 3, at % 3] = value[4 * half : 4 * half + 4]


def taken(totals, tile):
    return jnp.concatenate(
        [totals[at // 3, at % 3] for at in (2 * tile, 2 * tile + 1)], axis=0
    )


def prepare(offsets, kinds, rows, mass, table, mass_split, held):
    for b in range(NB):
        moved = pltpu.roll(rows[...], offsets[b], axis=1)
        for q in range(RECORD // 128):
            held[q, pl.ds(b, 2 * GROUP * GROUPS, stride=NB), :] = moved[:, q * 128 : (q + 1) * 128]
    for q in range(RECORD // 128):
        table[:, q * 128 : (q + 1) * 128] = held[q, :ROWS, :].astype(jnp.bfloat16)
    none = jnp.zeros((64, 64), jnp.float32)
    whole = jnp.concatenate(
        [
            jnp.concatenate([mass[kinds[0]], none], axis=1),
            jnp.concatenate([none, mass[kinds[1]]], axis=1),
        ],
        axis=0,
    )
    high, low = halves(whole)
    for at in (0, PTS):
        mass_split[at : at + PTS, :PTS] = high
        mass_split[at : at + PTS, PTS:] = low


def project(record, basis, table, mass_split, spectra, products, low_part, weighted, spec_rows):
    spectra[ROWS:, :] = jnp.zeros((GROUPS * 128 - ROWS, FLAT), jnp.bfloat16)
    weighted[ROWS:, :] = jnp.zeros((GROUPS * 128 - ROWS, 2 * FLAT), jnp.bfloat16)
    for lo, hi in ((0, 256), (256, 512), (512, 640)):
        part = jnp.dot(table[...], record[:, lo:hi], preferred_element_type=jnp.float32)
        spectra[:ROWS, lo:hi], low_part[:, lo:hi] = halves(part)
        pairs = part.reshape(ROWS // 16, 2, 8, hi - lo)
        spec_rows[:, lo:hi] = pairs[:, 0].reshape(ROWS // 2, hi - lo).astype(jnp.bfloat16)
        spec_rows[:, FLAT + lo : FLAT + hi] = (
            pairs[:, 1].reshape(ROWS // 2, hi - lo).astype(jnp.bfloat16)
        )
    for v in range(NVAR):
        at = slice(v * PTS, (v + 1) * PTS)
        to = slice(FLAT + v * PTS, FLAT + (v + 1) * PTS)
        both = jnp.concatenate([spectra[:ROWS, at], low_part[:, at]], axis=1)
        both = jnp.dot(both, mass_split[...], preferred_element_type=jnp.float32)
        one = both[:, :PTS] + both[:, PTS:]
        weighted[:ROWS, at] = one.astype(jnp.bfloat16)
        pairs = one.reshape(ROWS // 16, 2, 8, PTS)
        turned = jnp.stack([pairs[:, 1], -pairs[:, 0]], axis=1).reshape(ROWS, PTS)
        weighted[:ROWS, to] = turned.astype(jnp.bfloat16)
    across = (((1,), (1,)), ((), ()))
    grams = []
    place = lanes((RANK, 128)) // 16
    for g in range(GROUPS):
        count = min(GROUP, F - g * GROUP)
        fs = slice(g * GROUP, g * GROUP + count)
        right = weighted[g * 128 : (g + 1) * 128, :]
        modes = jnp.concatenate(
            [basis[c, fs, v].reshape(count * RANK, PTS) for c in range(2) for v in range(NVAR)],
            axis=1,
        )
        rows = max(count * NB, 16)
        own = spec_rows[g * 64 : g * 64 + rows, :]
        left = jnp.concatenate([modes, own], axis=0)
        both = lax.dot_general(left, right, across, preferred_element_type=jnp.float32)
        on_modes, on_own = both[: count * RANK], both[count * RANK :]
        kept_modes = jnp.zeros((RANK, 128), jnp.float32)
        kept_own = jnp.zeros((NB, 128), jnp.float32)
        for i in range(count):
            kept_modes = jnp.where(place == i, on_modes[i * RANK : (i + 1) * RANK], kept_modes)
            kept_own = jnp.where(place[:NB] == i, on_own[i * NB : (i + 1) * NB], kept_own)
        if g < GROUPS - 1:
            put(products, 2 * g, kept_modes[:8])
            put(products, 2 * g + 1, kept_modes[8:])
            grams.append(kept_own)
    upper = part_of((8, 128), 1) % 8 >= lax.broadcasted_iota(jnp.int32, (8, 128), 0)
    real = part_of((8, 128), 8) % 2 == 0
    for g in (0, 2):
        first = jnp.where(upper, grams[g], pltpu.roll(grams[g], 120, axis=1))
        second = jnp.where(upper, pltpu.roll(grams[g + 1], 8, axis=1), grams[g + 1])
        put(products, 8 + g // 2, jnp.where(real, first, second))
    last = jnp.where(upper, kept_own, pltpu.roll(kept_own, 120, axis=1))
    where = part_of((8, 128), 8)
    tile = jnp.where(where < 2, kept_modes[:8], 0.0)
    tile = jnp.where(where // 2 == 1, pltpu.roll(kept_modes[8:], 16, axis=1), tile)
    tile = jnp.where(where == 4, pltpu.roll(last, 32, axis=1), tile)
    put(products, 10, tile)
    put(products, 11, jnp.zeros((8, 128), jnp.float32))


def swapped(value):
    real = lanes(value.shape) // 8 % 2 == 0
    return jnp.where(real, pltpu.roll(value, 120, axis=1), pltpu.roll(value, 8, axis=1))


def signed(value):
    real = lanes(value.shape) // 8 % 2 == 0
    return jnp.where(real, value, -value)


def update(entries, totals, spectra, coeffs, out, ordered, staged, sems):
    place = lanes((RANK, 128)) // 16
    row_place = lax.broadcasted_iota(jnp.int32, (256, 128), 0) // 16 % 8
    same = (row_place == lanes((256, 128)) // 16).astype(jnp.bfloat16)
    exact, rounded, terms = [], [], []
    row = lax.broadcasted_iota(jnp.int32, (8, 128), 0)
    column = lanes((8, 128)) % 8
    real = part_of((8, 128), 8) % 2 == 0
    upper = jnp.where(column == row, 1.0, jnp.where(column > row, 2.0, 0.0))
    lower = jnp.where(column < row, 2.0, 0.0)
    on_real = jnp.where(real, upper, -lower)
    on_imag = jnp.where(real, lower, upper)
    last = taken(totals, 10)
    for g in range(GROUPS):
        if g < GROUPS - 1:
            coeff = jnp.concatenate([taken(totals, 2 * g), taken(totals, 2 * g + 1)], axis=0)
            gram = taken(totals, 8 + g // 2)
        else:
            coeff = jnp.concatenate([last, pltpu.roll(last, 112, axis=1)], axis=0)
            coeff = jnp.where(place == 0, coeff, 0.0)
            gram = pltpu.roll(last, 96, axis=1)
        if g % 2 == 0:
            gram = jnp.where(real, gram, pltpu.roll(gram, 8, axis=1))
        else:
            gram = jnp.where(real, pltpu.roll(gram, 120, axis=1), gram)
        coeff = coeff * (1.0 / math.sqrt(entries))
        exact.append(coeff)
        short = coeff.astype(jnp.bfloat16)
        coeff = short.astype(jnp.float32)
        rounded.append(coeff)
        first, second = gram * on_real, gram * on_imag
        tiles = []
        for i in range(GROUP):
            tiles += [
                jnp.where(place[:8] == i, first, 0.0),
                jnp.where(place[:8] == i, second, 0.0),
            ]
        pair = jnp.concatenate(halves(jnp.concatenate(tiles, axis=0)), axis=0)
        applied = jnp.dot(
            jnp.concatenate([short, short], axis=1), pair, preferred_element_type=jnp.float32
        )
        terms.append(coeff * applied)
    copies = []
    lane = lanes((8, 128))
    for c in range(2):
        for b in range(NB):
            index = lane % 8 * 16 + c * 8 + b
            for half in range(2):
                line = jnp.zeros((8, 128), jnp.float32)
                for g in range(GROUPS):
                    moved = jnp.take_along_axis(
                        exact[g][half * 8 : half * 8 + 8], index, axis=1, mode="promise_in_bounds"
                    )
                    line = jnp.where(lane // 8 == g, moved, line)
                ordered[c, b, half * 8 : half * 8 + 8, :] = line[:, :F]
    copy = pltpu.make_async_copy(ordered, coeffs, sems.at[2 * GROUPS])
    copy.start()
    copies.append(copy)
    terms = jnp.concatenate(halves(jnp.concatenate(terms, axis=0)), axis=1)
    energy = jnp.dot(terms, same, preferred_element_type=jnp.float32)
    factor = 1.0 / jnp.sqrt(jnp.maximum(energy, 0.0) / entries + 1e-06)
    for g in range(GROUPS):
        count = min(GROUP, F - g * GROUP)
        real, imag = signed(rounded[g]), swapped(rounded[g])
        left = []
        for i in range(count):
            left += [jnp.where(place == i, real, 0.0), jnp.where(place == i, imag, 0.0)]
        left = jnp.concatenate(left, axis=0).astype(jnp.bfloat16)
        right = spectra[g * 128 : (g + 1) * 128, :]
        fields = jnp.dot(left, right, preferred_element_type=jnp.float32)
        for i in range(count):
            scale = factor[g * RANK : (g + 1) * RANK, i * 16 : i * 16 + 1]
            scale = jnp.broadcast_to(scale, (RANK, PTS))
            for c in range(2):
                row = (2 * i + c) * RANK
                for v in range(NVAR):
                    one = fields[row : row + RANK, v * PTS : (v + 1) * PTS] * scale
                    staged[c, g * GROUP + i, v] = one.astype(jnp.bfloat16)
        for c in range(2):
            fs = pl.ds(g * GROUP, count)
            copy = pltpu.make_async_copy(staged.at[c, fs], out.at[c, fs], sems.at[2 * g + c])
            copy.start()
            copies.append(copy)
    for copy in copies:
        copy.wait()


def in_vmem(count):
    return [pl.BlockSpec(memory_space=pltpu.VMEM)] * count


def in_smem(count):
    return [pl.BlockSpec(memory_space=pltpu.SMEM)] * count


def params(mib):
    return pltpu.CompilerParams(vmem_limit_bytes=mib * 1024 * 1024)


def anywhere(count):
    return [pl.BlockSpec(memory_space=pl.ANY)] * count


def sent(snapshots):
    return pl.pallas_call(
        spread,
        out_shape=jax.ShapeDtypeStruct((64, NVAR, 8, PTS), jnp.bfloat16),
        in_specs=anywhere(1),
        out_specs=anywhere(1)[0],
        scratch_shapes=[pltpu.SemaphoreType.DMA((NVAR,))],
        compiler_params=params(2),
        name="send_order",
    )(snapshots)


def prepared(offsets, kinds, mass):
    return pl.pallas_call(
        prepare,
        out_shape=(
            jax.ShapeDtypeStruct((ROWS, RECORD), jnp.bfloat16),
            jax.ShapeDtypeStruct((2 * PTS, 2 * PTS), jnp.bfloat16),
        ),
        in_specs=in_smem(2) + in_vmem(2),
        out_specs=tuple(in_vmem(2)),
        scratch_shapes=[
            pltpu.VMEM((RECORD // 128, 2 * NB * GROUP * GROUPS, 128), jnp.float32)
        ],
        compiler_params=params(12),
        name="tables",
    )(offsets, kinds, jnp.asarray(window_rows()), mass)


def projected(record, basis, table, mass_split):
    return pl.pallas_call(
        project,
        out_shape=(
            jax.ShapeDtypeStruct((GROUPS * 128, FLAT), jnp.bfloat16),
            jax.ShapeDtypeStruct(SHARE, jnp.float32),
        ),
        in_specs=in_vmem(4),
        out_specs=tuple(in_vmem(2)),
        scratch_shapes=[
            pltpu.VMEM((ROWS, FLAT), jnp.bfloat16),
            pltpu.VMEM((GROUPS * 128, 2 * FLAT), jnp.bfloat16),
            pltpu.VMEM((ROWS // 2, 2 * FLAT), jnp.bfloat16),
        ],
        compiler_params=params(20),
        name="spectra_products",
    )(record, basis, table, mass_split)


def updated(entries, totals, spectra):
    shape = (2, F, NVAR, RANK, PTS)
    line = (2, NB, RANK, F)
    return pl.pallas_call(
        functools.partial(update, entries),
        out_shape=(
            jax.ShapeDtypeStruct(line, jnp.float32),
            jax.ShapeDtypeStruct(shape, jnp.bfloat16),
        ),
        in_specs=in_vmem(2),
        out_specs=tuple(anywhere(2)),
        scratch_shapes=[
            pltpu.VMEM(line, jnp.float32),
            pltpu.VMEM(shape, jnp.bfloat16),
            pltpu.SemaphoreType.DMA((2 * GROUPS + 1,)),
        ],
        compiler_params=params(20),
        name="fields_update",
    )(totals, spectra)


def exchanged(parts, axes):
    return lax.all_to_all(parts, axes, split_axis=0, concat_axis=0, tiled=True)


def sent_to_all(value, axes):
    size = math.prod(lax.axis_size(a) for a in axes)
    return exchanged(jnp.broadcast_to(value[None], (size, *value.shape)), axes)


def on_device(snapshots, basis, mass_table, elem_kind, offsets):
    lines = snapshots.transpose(1, 0, 2).reshape(NVAR, 8, 64, PTS).transpose(0, 2, 1, 3)
    arrived = exchanged(sent(lines), TM)
    record = arrived.transpose(0, 2, 1, 3).reshape(RECORD, FLAT)
    table, mass_split = prepared(offsets, elem_kind, mass_table)
    spectra, products = projected(record, basis.transpose(0, 1, 3, 2, 4), table, mass_split)
    own = exchanged(products, NEAR).sum(axis=0)
    own = sent_to_all(own.astype(jnp.bfloat16), FAR).astype(jnp.float32).sum(axis=0)
    totals = sent_to_all(own, NEAR)
    entries = FLAT * lax.axis_size(TM) * lax.axis_size("space")
    coeffs, new_basis = updated(entries, totals, spectra)
    return (coeffs.transpose(0, 3, 1, 2), new_basis.transpose(0, 1, 3, 2, 4))


def solution(mesh):
    finer = Mesh(
        mesh.devices.reshape(4, 8, 2, mesh.shape["space"]), ("tm_0", "tm_1", "tm_2", "space")
    )
    return jax.shard_map(
        on_device,
        mesh=finer,
        in_specs=(P(TM, None, "space"), P(None, None, None, None, SPACE_TM), P(), P(SPACE_TM), P()),
        out_specs=(P(), P(None, None, None, None, SPACE_TM)),
        check_vma=False,
    )
```

```python
import functools
import math

import jax
import jax.numpy as jnp
import numpy as np
from jax import lax
from jax.experimental import pallas as pl
from jax.experimental.pallas import tpu as pltpu
from jax.sharding import Mesh
from jax.sharding import PartitionSpec as P

NT = 256
TM = ("tm_0", "tm_1", "tm_2")
SPACE_TM = ("space_0", "space_1", "tm_0", "tm_1", "tm_2")
NEAR = ("tm_2", "tm_0", "space_1")
FAR = ("tm_1", "space_0")

F = 33
NB = 8
RANK = 16
NVAR = 5
PTS = 128
RECORD = 512
GROUP = 8
GROUPS = 5
ROWS = 544
FLAT = NVAR * PTS
SHARE = (16, 3, 2, 128)


def window_rows():
    j = np.arange(NT)
    weight = (0.5 - 0.5 * np.cos(2 * np.pi * j / NT)) / math.sqrt(0.375 * NT)
    angle = 2 * np.pi * (np.arange(F)[:, None] * j % NT) / NT
    rows = np.stack([weight * np.cos(angle), -weight * np.sin(angle)], axis=1)
    out = np.zeros((2 * GROUP * GROUPS, RECORD), np.float32)
    out[: 2 * F, :NT] = rows.reshape(2 * F, NT)
    return out


def lanes(shape):
    return lax.broadcasted_iota(jnp.int32, shape, len(shape) - 1)


def spread(snapshots, parts, sems):
    copies = []
    for v in range(NVAR):
        copy = pltpu.make_async_copy(snapshots.at[v], parts.at[:, v], sems.at[v])
        copy.start()
        copies.append(copy)
    for copy in copies:
        copy.wait()


def halves(value):
    high = value.astype(jnp.bfloat16)
    return high, (value - high.astype(jnp.float32)).astype(jnp.bfloat16)


def part_of(shape, size):
    return lanes(shape) // size


def put(products, tile, value):
    size = SHARE[2]
    for i in range(8 // size):
        at = tile * (8 // size) + i
        products[at // 3, at % 3] = value[size * i : size * (i + 1)]


def taken(totals, tile):
    count = 8 // SHARE[2]
    return jnp.concatenate(
        [totals[at // 3, at % 3] for at in range(tile * count, (tile + 1) * count)], axis=0
    )


def prepare(offsets, kinds, rows, mass, table, mass_split, held):
    for b in range(NB):
        moved = pltpu.roll(rows[...], offsets[b], axis=1)
        for q in range(RECORD // 128):
            held[q, pl.ds(b, 2 * GROUP * GROUPS, stride=NB), :] = moved[:, q * 128 : (q + 1) * 128]
    for q in range(RECORD // 128):
        table[:, q * 128 : (q + 1) * 128] = held[q, :ROWS, :].astype(jnp.bfloat16)
    none = jnp.zeros((64, 64), jnp.float32)
    whole = jnp.concatenate(
        [
            jnp.concatenate([mass[kinds[0]], none], axis=1),
            jnp.concatenate([none, mass[kinds[1]]], axis=1),
        ],
        axis=0,
    )
    high, low = halves(whole)
    for at in (0, PTS):
        mass_split[at : at + PTS, :PTS] = high
        mass_split[at : at + PTS, PTS:] = low


def project(record, basis, table, mass_split, spectra, products, low_part, weighted, spec_rows):
    spectra[ROWS:, :] = jnp.zeros((GROUPS * 128 - ROWS, FLAT), jnp.bfloat16)
    weighted[ROWS:, :] = jnp.zeros((GROUPS * 128 - ROWS, 2 * FLAT), jnp.bfloat16)
    for lo, hi in ((0, 256), (256, 512), (512, 640)):
        part = jnp.dot(table[...], record[:, lo:hi], preferred_element_type=jnp.float32)
        spectra[:ROWS, lo:hi], low_part[:, lo:hi] = halves(part)
        pairs = part.reshape(ROWS // 16, 2, 8, hi - lo)
        spec_rows[:, lo:hi] = pairs[:, 0].reshape(ROWS // 2, hi - lo).astype(jnp.bfloat16)
        spec_rows[:, FLAT + lo : FLAT + hi] = (
            pairs[:, 1].reshape(ROWS // 2, hi - lo).astype(jnp.bfloat16)
        )
    for v in range(NVAR):
        at = slice(v * PTS, (v + 1) * PTS)
        to = slice(FLAT + v * PTS, FLAT + (v + 1) * PTS)
        both = jnp.concatenate([spectra[:ROWS, at], low_part[:, at]], axis=1)
        both = jnp.dot(both, mass_split[...], preferred_element_type=jnp.float32)
        one = both[:, :PTS] + both[:, PTS:]
        weighted[:ROWS, at] = one.astype(jnp.bfloat16)
        pairs = one.reshape(ROWS // 16, 2, 8, PTS)
        turned = jnp.stack([pairs[:, 1], -pairs[:, 0]], axis=1).reshape(ROWS, PTS)
        weighted[:ROWS, to] = turned.astype(jnp.bfloat16)
    across = (((1,), (1,)), ((), ()))
    grams = []
    place = lanes((RANK, 128)) // 16
    for g in range(GROUPS):
        count = min(GROUP, F - g * GROUP)
        fs = slice(g * GROUP, g * GROUP + count)
        right = weighted[g * 128 : (g + 1) * 128, :]
        modes = jnp.concatenate(
            [basis[c, fs, v].reshape(count * RANK, PTS) for c in range(2) for v in range(NVAR)],
            axis=1,
        )
        rows = max(count * NB, 16)
        own = spec_rows[g * 64 : g * 64 + rows, :]
        left = jnp.concatenate([modes, own], axis=0)
        both = lax.dot_general(left, right, across, preferred_element_type=jnp.float32)
        on_modes, on_own = both[: count * RANK], both[count * RANK :]
        kept_modes = jnp.zeros((RANK, 128), jnp.float32)
        kept_own = jnp.zeros((NB, 128), jnp.float32)
        for i in range(count):
            kept_modes = jnp.where(place == i, on_modes[i * RANK : (i + 1) * RANK], kept_modes)
            kept_own = jnp.where(place[:NB] == i, on_own[i * NB : (i + 1) * NB], kept_own)
        if g < GROUPS - 1:
            put(products, 2 * g, kept_modes[:8])
            put(products, 2 * g + 1, kept_modes[8:])
            grams.append(kept_own)
    upper = part_of((8, 128), 1) % 8 >= lax.broadcasted_iota(jnp.int32, (8, 128), 0)
    real = part_of((8, 128), 8) % 2 == 0
    for g in (0, 2):
        first = jnp.where(upper, grams[g], pltpu.roll(grams[g], 120, axis=1))
        second = jnp.where(upper, pltpu.roll(grams[g + 1], 8, axis=1), grams[g + 1])
        put(products, 8 + g // 2, jnp.where(real, first, second))
    last = jnp.where(upper, kept_own, pltpu.roll(kept_own, 120, axis=1))
    where = part_of((8, 128), 8)
    tile = jnp.where(where < 2, kept_modes[:8], 0.0)
    tile = jnp.where(where // 2 == 1, pltpu.roll(kept_modes[8:], 16, axis=1), tile)
    tile = jnp.where(where == 4, pltpu.roll(last, 32, axis=1), tile)
    put(products, 10, tile)
    put(products, 11, jnp.zeros((8, 128), jnp.float32))


def swapped(value):
    real = lanes(value.shape) // 8 % 2 == 0
    return jnp.where(real, pltpu.roll(value, 120, axis=1), pltpu.roll(value, 8, axis=1))


def signed(value):
    real = lanes(value.shape) // 8 % 2 == 0
    return jnp.where(real, value, -value)


def update(entries, totals, spectra, coeffs, out, ordered, staged, sems):
    place = lanes((RANK, 128)) // 16
    row_place = lax.broadcasted_iota(jnp.int32, (256, 128), 0) // 16 % 8
    same = (row_place == lanes((256, 128)) // 16).astype(jnp.bfloat16)
    exact, rounded, terms = [], [], []
    row = lax.broadcasted_iota(jnp.int32, (8, 128), 0)
    column = lanes((8, 128)) % 8
    real = part_of((8, 128), 8) % 2 == 0
    upper = jnp.where(column == row, 1.0, jnp.where(column > row, 2.0, 0.0))
    lower = jnp.where(column < row, 2.0, 0.0)
    on_real = jnp.where(real, upper, -lower)
    on_imag = jnp.where(real, lower, upper)
    last = taken(totals, 10)
    for g in range(GROUPS):
        if g < GROUPS - 1:
            coeff = jnp.concatenate([taken(totals, 2 * g), taken(totals, 2 * g + 1)], axis=0)
            gram = taken(totals, 8 + g // 2)
        else:
            coeff = jnp.concatenate([last, pltpu.roll(last, 112, axis=1)], axis=0)
            coeff = jnp.where(place == 0, coeff, 0.0)
            gram = pltpu.roll(last, 96, axis=1)
        if g % 2 == 0:
            gram = jnp.where(real, gram, pltpu.roll(gram, 8, axis=1))
        else:
            gram = jnp.where(real, pltpu.roll(gram, 120, axis=1), gram)
        coeff = coeff * (1.0 / math.sqrt(entries))
        exact.append(coeff)
        short = coeff.astype(jnp.bfloat16)
        coeff = short.astype(jnp.float32)
        rounded.append(coeff)
        first, second = gram * on_real, gram * on_imag
        tiles = []
        for i in range(GROUP):
            tiles += [
                jnp.where(place[:8] == i, first, 0.0),
                jnp.where(place[:8] == i, second, 0.0),
            ]
        pair = jnp.concatenate(halves(jnp.concatenate(tiles, axis=0)), axis=0)
        applied = jnp.dot(
            jnp.concatenate([short, short], axis=1), pair, preferred_element_type=jnp.float32
        )
        terms.append(coeff * applied)
    copies = []
    lane = lanes((8, 128))
    for c in range(2):
        for b in range(NB):
            index = lane % 8 * 16 + c * 8 + b
            for half in range(2):
                line = jnp.zeros((8, 128), jnp.float32)
                for g in range(GROUPS):
                    moved = jnp.take_along_axis(
                        exact[g][half * 8 : half * 8 + 8], index, axis=1, mode="promise_in_bounds"
                    )
                    line = jnp.where(lane // 8 == g, moved, line)
                ordered[c, b, half * 8 : half * 8 + 8, :] = line[:, :F]
    copy = pltpu.make_async_copy(ordered, coeffs, sems.at[2 * GROUPS])
    copy.start()
    copies.append(copy)
    terms = jnp.concatenate(halves(jnp.concatenate(terms, axis=0)), axis=1)
    energy = jnp.dot(terms, same, preferred_element_type=jnp.float32)
    factor = 1.0 / jnp.sqrt(jnp.maximum(energy, 0.0) / entries + 1e-06)
    for g in range(GROUPS):
        count = min(GROUP, F - g * GROUP)
        real, imag = signed(rounded[g]), swapped(rounded[g])
        left = []
        for i in range(count):
            left += [jnp.where(place == i, real, 0.0), jnp.where(place == i, imag, 0.0)]
        left = jnp.concatenate(left, axis=0).astype(jnp.bfloat16)
        right = spectra[g * 128 : (g + 1) * 128, :]
        fields = jnp.dot(left, right, preferred_element_type=jnp.float32)
        for i in range(count):
            scale = factor[g * RANK : (g + 1) * RANK, i * 16 : i * 16 + 1]
            scale = jnp.broadcast_to(scale, (RANK, PTS))
            for c in range(2):
                row = (2 * i + c) * RANK
                for v in range(NVAR):
                    one = fields[row : row + RANK, v * PTS : (v + 1) * PTS] * scale
                    staged[c, g * GROUP + i, v] = one.astype(jnp.bfloat16)
        for c in range(2):
            fs = pl.ds(g * GROUP, count)
            copy = pltpu.make_async_copy(staged.at[c, fs], out.at[c, fs], sems.at[2 * g + c])
            copy.start()
            copies.append(copy)
    for copy in copies:
        copy.wait()


def in_vmem(count):
    return [pl.BlockSpec(memory_space=pltpu.VMEM)] * count


def in_smem(count):
    return [pl.BlockSpec(memory_space=pltpu.SMEM)] * count


def params(mib):
    return pltpu.CompilerParams(vmem_limit_bytes=mib * 1024 * 1024)


def anywhere(count):
    return [pl.BlockSpec(memory_space=pl.ANY)] * count


def sent(snapshots):
    return pl.pallas_call(
        spread,
        out_shape=jax.ShapeDtypeStruct((64, NVAR, 8, PTS), jnp.bfloat16),
        in_specs=anywhere(1),
        out_specs=anywhere(1)[0],
        scratch_shapes=[pltpu.SemaphoreType.DMA((NVAR,))],
        compiler_params=params(2),
        name="send_order",
    )(snapshots)


def prepared(offsets, kinds, mass):
    return pl.pallas_call(
        prepare,
        out_shape=(
            jax.ShapeDtypeStruct((ROWS, RECORD), jnp.bfloat16),
            jax.ShapeDtypeStruct((2 * PTS, 2 * PTS), jnp.bfloat16),
        ),
        in_specs=in_smem(2) + in_vmem(2),
        out_specs=tuple(in_vmem(2)),
        scratch_shapes=[
            pltpu.VMEM((RECORD // 128, 2 * NB * GROUP * GROUPS, 128), jnp.float32)
        ],
        compiler_params=params(12),
        name="tables",
    )(offsets, kinds, jnp.asarray(window_rows()), mass)


def projected(record, basis, table, mass_split):
    return pl.pallas_call(
        project,
        out_shape=(
            jax.ShapeDtypeStruct((GROUPS * 128, FLAT), jnp.bfloat16),
            jax.ShapeDtypeStruct(SHARE, jnp.float32),
        ),
        in_specs=in_vmem(4),
        out_specs=tuple(in_vmem(2)),
        scratch_shapes=[
            pltpu.VMEM((ROWS, FLAT), jnp.bfloat16),
            pltpu.VMEM((GROUPS * 128, 2 * FLAT), jnp.bfloat16),
            pltpu.VMEM((ROWS // 2, 2 * FLAT), jnp.bfloat16),
        ],
        compiler_params=params(20),
        name="spectra_products",
    )(record, basis, table, mass_split)


def updated(entries, totals, spectra):
    shape = (2, F, NVAR, RANK, PTS)
    line = (2, NB, RANK, F)
    return pl.pallas_call(
        functools.partial(update, entries),
        out_shape=(
            jax.ShapeDtypeStruct(line, jnp.float32),
            jax.ShapeDtypeStruct(shape, jnp.bfloat16),
        ),
        in_specs=in_vmem(2),
        out_specs=tuple(anywhere(2)),
        scratch_shapes=[
            pltpu.VMEM(line, jnp.float32),
            pltpu.VMEM(shape, jnp.bfloat16),
            pltpu.SemaphoreType.DMA((2 * GROUPS + 1,)),
        ],
        compiler_params=params(20),
        name="fields_update",
    )(totals, spectra)


def exchanged(parts, axes):
    return lax.all_to_all(parts, axes, split_axis=0, concat_axis=0, tiled=True)


def sent_to_all(value, axes):
    size = math.prod(lax.axis_size(a) for a in axes)
    return exchanged(jnp.broadcast_to(value[None], (size, *value.shape)), axes)


def on_device(snapshots, basis, mass_table, elem_kind, offsets):
    lines = snapshots.transpose(1, 0, 2).reshape(NVAR, 8, 64, PTS).transpose(0, 2, 1, 3)
    arrived = exchanged(sent(lines), TM)
    record = arrived.transpose(0, 2, 1, 3).reshape(RECORD, FLAT)
    table, mass_split = prepared(offsets, elem_kind, mass_table)
    spectra, products = projected(record, basis.transpose(0, 1, 3, 2, 4), table, mass_split)
    own = exchanged(products, NEAR).sum(axis=0)
    own = sent_to_all(own, FAR).sum(axis=0)
    totals = sent_to_all(own, NEAR)
    entries = FLAT * lax.axis_size(TM) * lax.axis_size(("space_0", "space_1"))
    coeffs, new_basis = updated(entries, totals, spectra)
    return (coeffs.transpose(0, 3, 1, 2), new_basis.transpose(0, 1, 3, 2, 4))


def solution(mesh):
    finer = Mesh(
        mesh.devices.reshape(4, 8, 2, 4, 2), ("tm_0", "tm_1", "tm_2", "space_0", "space_1")
    )
    return jax.shard_map(
        on_device,
        mesh=finer,
        in_specs=(P(TM, None, ("space_0", "space_1")), P(None, None, None, None, SPACE_TM), P(), P(SPACE_TM), P()),
        out_specs=(P(), P(None, None, None, None, SPACE_TM)),
        check_vma=False,
    )
```

```python
import functools
import math

import jax
import jax.numpy as jnp
import numpy as np
from jax import lax
from jax.experimental import pallas as pl
from jax.experimental.pallas import tpu as pltpu
from jax.sharding import Mesh
from jax.sharding import PartitionSpec as P

NT = 256
TM = ("tm_0", "tm_1", "tm_2")
SPACE_TM = ("space_0", "space_1", "tm_0", "tm_1", "tm_2")
NEAR = ("tm_2", "tm_0", "space_1")
FAR = ("tm_1", "space_0")

F = 33
NB = 8
RANK = 16
NVAR = 5
PTS = 128
RECORD = 512
GROUP = 8
GROUPS = 5
ROWS = 544
FLAT = NVAR * PTS
SHARE = (16, 3, 2, 128)


def window_rows():
    j = np.arange(NT)
    weight = (0.5 - 0.5 * np.cos(2 * np.pi * j / NT)) / math.sqrt(0.375 * NT)
    angle = 2 * np.pi * (np.arange(F)[:, None] * j % NT) / NT
    rows = np.stack([weight * np.cos(angle), -weight * np.sin(angle)], axis=1)
    out = np.zeros((2 * GROUP * GROUPS, RECORD), np.float32)
    out[: 2 * F, :NT] = rows.reshape(2 * F, NT)
    return out


def lanes(shape):
    return lax.broadcasted_iota(jnp.int32, shape, len(shape) - 1)


def spread(snapshots, parts, sems):
    copies = []
    for v in range(NVAR):
        copy = pltpu.make_async_copy(snapshots.at[v], parts.at[:, v], sems.at[v])
        copy.start()
        copies.append(copy)
    for copy in copies:
        copy.wait()


def halves(value):
    high = value.astype(jnp.bfloat16)
    return high, (value - high.astype(jnp.float32)).astype(jnp.bfloat16)


def part_of(shape, size):
    return lanes(shape) // size


def put(products, tile, value):
    size = SHARE[2]
    for i in range(8 // size):
        at = tile * (8 // size) + i
        products[at // 3, at % 3] = value[size * i : size * (i + 1)]


def taken(totals, tile):
    count = 8 // SHARE[2]
    return jnp.concatenate(
        [totals[at // 3, at % 3] for at in range(tile * count, (tile + 1) * count)], axis=0
    )


def prepare(offsets, kinds, rows, mass, table, mass_split, held):
    for b in range(NB):
        moved = pltpu.roll(rows[...], offsets[b], axis=1)
        for q in range(RECORD // 128):
            held[q, pl.ds(b, 2 * GROUP * GROUPS, stride=NB), :] = moved[:, q * 128 : (q + 1) * 128]
    for q in range(RECORD // 128):
        table[:, q * 128 : (q + 1) * 128] = held[q, :ROWS, :].astype(jnp.bfloat16)
    none = jnp.zeros((64, 64), jnp.float32)
    whole = jnp.concatenate(
        [
            jnp.concatenate([mass[kinds[0]], none], axis=1),
            jnp.concatenate([none, mass[kinds[1]]], axis=1),
        ],
        axis=0,
    )
    high, low = halves(whole)
    for at in (0, PTS):
        mass_split[at : at + PTS, :PTS] = high
        mass_split[at : at + PTS, PTS:] = low


def project(record, basis, table, mass_split, spectra, products, low_part, weighted, spec_rows):
    spectra[ROWS:, :] = jnp.zeros((GROUPS * 128 - ROWS, FLAT), jnp.bfloat16)
    weighted[ROWS:, :] = jnp.zeros((GROUPS * 128 - ROWS, 2 * FLAT), jnp.bfloat16)
    for lo, hi in ((0, 256), (256, 512), (512, 640)):
        part = jnp.dot(table[...], record[:, lo:hi], preferred_element_type=jnp.float32)
        spectra[:ROWS, lo:hi], low_part[:, lo:hi] = halves(part)
        pairs = part.reshape(ROWS // 16, 2, 8, hi - lo)
        spec_rows[:, lo:hi] = pairs[:, 0].reshape(ROWS // 2, hi - lo).astype(jnp.bfloat16)
        spec_rows[:, FLAT + lo : FLAT + hi] = (
            pairs[:, 1].reshape(ROWS // 2, hi - lo).astype(jnp.bfloat16)
        )
    for v in range(NVAR):
        at = slice(v * PTS, (v + 1) * PTS)
        to = slice(FLAT + v * PTS, FLAT + (v + 1) * PTS)
        both = jnp.concatenate([spectra[:ROWS, at], low_part[:, at]], axis=1)
        both = jnp.dot(both, mass_split[...], preferred_element_type=jnp.float32)
        one = both[:, :PTS] + both[:, PTS:]
        weighted[:ROWS, at] = one.astype(jnp.bfloat16)
        pairs = one.reshape(ROWS // 16, 2, 8, PTS)
        turned = jnp.stack([pairs[:, 1], -pairs[:, 0]], axis=1).reshape(ROWS, PTS)
        weighted[:ROWS, to] = turned.astype(jnp.bfloat16)
    across = (((1,), (1,)), ((), ()))
    grams = []
    place = lanes((RANK, 128)) // 16
    for g in range(GROUPS):
        count = min(GROUP, F - g * GROUP)
        fs = slice(g * GROUP, g * GROUP + count)
        right = weighted[g * 128 : (g + 1) * 128, :]
        modes = jnp.concatenate(
            [basis[c, fs, v].reshape(count * RANK, PTS) for c in range(2) for v in range(NVAR)],
            axis=1,
        )
        rows = max(count * NB, 16)
        own = spec_rows[g * 64 : g * 64 + rows, :]
        left = jnp.concatenate([modes, own], axis=0)
        both = lax.dot_general(left, right, across, preferred_element_type=jnp.float32)
        on_modes, on_own = both[: count * RANK], both[count * RANK :]
        kept_modes = jnp.zeros((RANK, 128), jnp.float32)
        kept_own = jnp.zeros((NB, 128), jnp.float32)
        for i in range(count):
            kept_modes = jnp.where(place == i, on_modes[i * RANK : (i + 1) * RANK], kept_modes)
            kept_own = jnp.where(place[:NB] == i, on_own[i * NB : (i + 1) * NB], kept_own)
        if g < GROUPS - 1:
            put(products, 2 * g, kept_modes[:8])
            put(products, 2 * g + 1, kept_modes[8:])
            grams.append(kept_own)
    upper = part_of((8, 128), 1) % 8 >= lax.broadcasted_iota(jnp.int32, (8, 128), 0)
    real = part_of((8, 128), 8) % 2 == 0
    for g in (0, 2):
        first = jnp.where(upper, grams[g], pltpu.roll(grams[g], 120, axis=1))
        second = jnp.where(upper, pltpu.roll(grams[g + 1], 8, axis=1), grams[g + 1])
        put(products, 8 + g // 2, jnp.where(real, first, second))
    last = jnp.where(upper, kept_own, pltpu.roll(kept_own, 120, axis=1))
    where = part_of((8, 128), 8)
    tile = jnp.where(where < 2, kept_modes[:8], 0.0)
    tile = jnp.where(where // 2 == 1, pltpu.roll(kept_modes[8:], 16, axis=1), tile)
    tile = jnp.where(where == 4, pltpu.roll(last, 32, axis=1), tile)
    put(products, 10, tile)
    put(products, 11, jnp.zeros((8, 128), jnp.float32))


def swapped(value):
    real = lanes(value.shape) // 8 % 2 == 0
    return jnp.where(real, pltpu.roll(value, 120, axis=1), pltpu.roll(value, 8, axis=1))


def signed(value):
    real = lanes(value.shape) // 8 % 2 == 0
    return jnp.where(real, value, -value)


def update(entries, totals, spectra, coeffs, out, ordered, staged, sems):
    place = lanes((RANK, 128)) // 16
    row_place = lax.broadcasted_iota(jnp.int32, (256, 128), 0) // 16 % 8
    same = (row_place == lanes((256, 128)) // 16).astype(jnp.bfloat16)
    exact, rounded, terms = [], [], []
    row = lax.broadcasted_iota(jnp.int32, (8, 128), 0)
    column = lanes((8, 128)) % 8
    real = part_of((8, 128), 8) % 2 == 0
    upper = jnp.where(column == row, 1.0, jnp.where(column > row, 2.0, 0.0))
    lower = jnp.where(column < row, 2.0, 0.0)
    on_real = jnp.where(real, upper, -lower)
    on_imag = jnp.where(real, lower, upper)
    last = taken(totals, 10)
    for g in range(GROUPS):
        if g < GROUPS - 1:
            coeff = jnp.concatenate([taken(totals, 2 * g), taken(totals, 2 * g + 1)], axis=0)
            gram = taken(totals, 8 + g // 2)
        else:
            coeff = jnp.concatenate([last, pltpu.roll(last, 112, axis=1)], axis=0)
            coeff = jnp.where(place == 0, coeff, 0.0)
            gram = pltpu.roll(last, 96, axis=1)
        if g % 2 == 0:
            gram = jnp.where(real, gram, pltpu.roll(gram, 8, axis=1))
        else:
            gram = jnp.where(real, pltpu.roll(gram, 120, axis=1), gram)
        coeff = coeff * (1.0 / math.sqrt(entries))
        exact.append(coeff)
        short = coeff.astype(jnp.bfloat16)
        coeff = short.astype(jnp.float32)
        rounded.append(coeff)
        first, second = gram * on_real, gram * on_imag
        tiles = []
        for i in range(GROUP):
            tiles += [
                jnp.where(place[:8] == i, first, 0.0),
                jnp.where(place[:8] == i, second, 0.0),
            ]
        pair = jnp.concatenate(halves(jnp.concatenate(tiles, axis=0)), axis=0)
        applied = jnp.dot(
            jnp.concatenate([short, short], axis=1), pair, preferred_element_type=jnp.float32
        )
        terms.append(coeff * applied)
    copies = []
    lane = lanes((8, 128))
    for c in range(2):
        for b in range(NB):
            index = lane % 8 * 16 + c * 8 + b
            for half in range(2):
                line = jnp.zeros((8, 128), jnp.float32)
                for g in range(GROUPS):
                    moved = jnp.take_along_axis(
                        exact[g][half * 8 : half * 8 + 8], index, axis=1, mode="promise_in_bounds"
                    )
                    line = jnp.where(lane // 8 == g, moved, line)
                ordered[c, b, half * 8 : half * 8 + 8, :] = line[:, :F]
    copy = pltpu.make_async_copy(ordered, coeffs, sems.at[GROUPS])
    copy.start()
    copies.append(copy)
    terms = jnp.concatenate(halves(jnp.concatenate(terms, axis=0)), axis=1)
    energy = jnp.dot(terms, same, preferred_element_type=jnp.float32)
    factor = 1.0 / jnp.sqrt(jnp.maximum(energy, 0.0) / entries + 1e-06)
    for g in range(GROUPS):
        count = min(GROUP, F - g * GROUP)
        real, imag = signed(rounded[g]), swapped(rounded[g])
        left = []
        for i in range(count):
            left += [jnp.where(place == i, real, 0.0), jnp.where(place == i, imag, 0.0)]
        left = jnp.concatenate(left, axis=0).astype(jnp.bfloat16)
        right = spectra[g * 128 : (g + 1) * 128, :]
        fields = jnp.dot(left, right, preferred_element_type=jnp.float32)
        for i in range(count):
            scale = factor[g * RANK : (g + 1) * RANK, i * 16 : i * 16 + 1]
            scale = jnp.broadcast_to(scale, (RANK, PTS))
            for c in range(2):
                row = (2 * i + c) * RANK
                for v in range(NVAR):
                    one = fields[row : row + RANK, v * PTS : (v + 1) * PTS] * scale
                    staged[c, g * GROUP + i, v] = one.astype(jnp.bfloat16)
        fs = pl.ds(g * GROUP, count)
        copy = pltpu.make_async_copy(staged.at[:, fs], out.at[:, fs], sems.at[g])
        copy.start()
        copies.append(copy)
    for copy in copies:
        copy.wait()


def in_vmem(count):
    return [pl.BlockSpec(memory_space=pltpu.VMEM)] * count


def in_smem(count):
    return [pl.BlockSpec(memory_space=pltpu.SMEM)] * count


def params(mib):
    return pltpu.CompilerParams(vmem_limit_bytes=mib * 1024 * 1024)


def anywhere(count):
    return [pl.BlockSpec(memory_space=pl.ANY)] * count


def sent(snapshots):
    return pl.pallas_call(
        spread,
        out_shape=jax.ShapeDtypeStruct((64, NVAR, 8, PTS), jnp.bfloat16),
        in_specs=anywhere(1),
        out_specs=anywhere(1)[0],
        scratch_shapes=[pltpu.SemaphoreType.DMA((NVAR,))],
        compiler_params=params(2),
        name="send_order",
    )(snapshots)


def prepared(offsets, kinds, mass):
    return pl.pallas_call(
        prepare,
        out_shape=(
            jax.ShapeDtypeStruct((ROWS, RECORD), jnp.bfloat16),
            jax.ShapeDtypeStruct((2 * PTS, 2 * PTS), jnp.bfloat16),
        ),
        in_specs=in_smem(2) + in_vmem(2),
        out_specs=tuple(in_vmem(2)),
        scratch_shapes=[
            pltpu.VMEM((RECORD // 128, 2 * NB * GROUP * GROUPS, 128), jnp.float32)
        ],
        compiler_params=params(12),
        name="tables",
    )(offsets, kinds, jnp.asarray(window_rows()), mass)


def projected(record, basis, table, mass_split):
    return pl.pallas_call(
        project,
        out_shape=(
            jax.ShapeDtypeStruct((GROUPS * 128, FLAT), jnp.bfloat16),
            jax.ShapeDtypeStruct(SHARE, jnp.float32),
        ),
        in_specs=in_vmem(4),
        out_specs=tuple(in_vmem(2)),
        scratch_shapes=[
            pltpu.VMEM((ROWS, FLAT), jnp.bfloat16),
            pltpu.VMEM((GROUPS * 128, 2 * FLAT), jnp.bfloat16),
            pltpu.VMEM((ROWS // 2, 2 * FLAT), jnp.bfloat16),
        ],
        compiler_params=params(20),
        name="spectra_products",
    )(record, basis, table, mass_split)


def updated(entries, totals, spectra):
    shape = (2, F, NVAR, RANK, PTS)
    line = (2, NB, RANK, F)
    return pl.pallas_call(
        functools.partial(update, entries),
        out_shape=(
            jax.ShapeDtypeStruct(line, jnp.float32),
            jax.ShapeDtypeStruct(shape, jnp.bfloat16),
        ),
        in_specs=in_vmem(2),
        out_specs=tuple(anywhere(2)),
        scratch_shapes=[
            pltpu.VMEM(line, jnp.float32),
            pltpu.VMEM(shape, jnp.bfloat16),
            pltpu.SemaphoreType.DMA((GROUPS + 1,)),
        ],
        compiler_params=params(20),
        name="fields_update",
    )(totals, spectra)


def exchanged(parts, axes):
    return lax.all_to_all(parts, axes, split_axis=0, concat_axis=0, tiled=True)


def sent_to_all(value, axes):
    size = math.prod(lax.axis_size(a) for a in axes)
    return exchanged(jnp.broadcast_to(value[None], (size, *value.shape)), axes)


def on_device(snapshots, basis, mass_table, elem_kind, offsets):
    lines = snapshots.transpose(1, 0, 2).reshape(NVAR, 8, 64, PTS).transpose(0, 2, 1, 3)
    arrived = exchanged(sent(lines), TM)
    record = arrived.transpose(0, 2, 1, 3).reshape(RECORD, FLAT)
    table, mass_split = prepared(offsets, elem_kind, mass_table)
    spectra, products = projected(record, basis.transpose(0, 1, 3, 2, 4), table, mass_split)
    own = exchanged(products, NEAR).sum(axis=0)
    own = sent_to_all(own, FAR).sum(axis=0)
    totals = sent_to_all(own, NEAR)
    entries = FLAT * lax.axis_size(TM) * lax.axis_size(("space_0", "space_1"))
    coeffs, new_basis = updated(entries, totals, spectra)
    return (coeffs.transpose(0, 3, 1, 2), new_basis.transpose(0, 1, 3, 2, 4))


def solution(mesh):
    finer = Mesh(
        mesh.devices.reshape(4, 8, 2, 4, 2), ("tm_0", "tm_1", "tm_2", "space_0", "space_1")
    )
    return jax.shard_map(
        on_device,
        mesh=finer,
        in_specs=(P(TM, None, ("space_0", "space_1")), P(None, None, None, None, SPACE_TM), P(), P(SPACE_TM), P()),
        out_specs=(P(), P(None, None, None, None, SPACE_TM)),
        check_vma=False,
    )
```
